32 devices in a mesh: groups: 2 (over x), expert: 16 (over z, y, core).
Axes of the slice: x: 2, y: 2, z: 4, core: 2. Of those that a mesh axis runs over, the one named last changes fastest.
Arguments:
- hidden: bfloat16 [2048, 4096], P(('groups', 'expert')), parts along dimension 0, may hold values from -6 to 6
- norm_gain: bfloat16 [4096], replicated, may hold values from 0.099609375 to 1.8984375
- routes: int32 [2048, 8], P(('groups', 'expert')), parts along dimension 0, may hold values from 0 to 7, as said below
- gate_vals: float32 [2048, 8], P(('groups', 'expert')), parts along dimension 0, may hold values from 0.02 to 0.3
- span_len: int32 [32], P('groups'), parts along dimension 0, may hold values from 33 to 64, as said below
- w_gate: bfloat16 [16, 4096, 768], P('expert'), may hold values from -0.09375 to 0.09375
- w_up: bfloat16 [16, 4096, 768], P('expert'), may hold values from -0.09375 to 0.09375
- w_down: bfloat16 [16, 768, 4096], P('expert'), may hold values from -0.15625 to 0.15625
Outputs:
- output: bfloat16 [2048, 4096], P(('groups', 'expert')), parts along dimension 0
The draws below stay inside these ranges and needn't reach their ends.
There are 2 independent parts, one for each index of `groups`. The reference program is written for one: setup_inputs(seed, part) draws one part's arguments, and reference() takes and returns one part's arrays. A program takes and returns all parts, laid end to end along the dimension named above; an argument that names none is the same for every part. Nothing has to cross between parts.
Inputs may be any that keep to these rules, and one draw needn't show every extreme that they name: `routes`: each row names 8 different experts. In the rows of one device no expert is named more than 64 times, live or not, and in every draw the live choices of some device name some expert exactly 64 times. `span_len`: in every draw some sequence has all 64 positions live.
All inputs are finite; a program needn't handle non-finite values.
Results may differ from the reference program's by a relative error of at most 0.0039.
Values may be sent and summed in bfloat16 or wider, within the bound.
A program may use at most 128 MiB of HBM per device.

```python
import math
import jax
import jax.numpy as jnp
from jax import lax

D = 4096
FF = 1536
TOPK = 8
TOK_DEV = 64
FF_HALF = 768
EXPERTS = 8
TOKENS = 1024
SEQ_TOK = 64
SEQS = 16
CAP = 64
N_EXPERT = 16


def draw_routes(key, part):
    key = jax.random.fold_in(key, 11)
    hottest_key, device_key = jax.random.split(key)
    others = EXPERTS - 1
    total_picks = TOK_DEV * TOPK
    remain = total_picks - CAP
    baseline = remain // others
    surplus = remain % others
    spread = max(0, min(baseline - 1, CAP - baseline - 2))
    pair_count = others // 2
    hottest = jax.random.randint(hottest_key, (), 0, EXPERTS, dtype=jnp.int32)

    def column_order(choice_key):
        return jax.random.permutation(choice_key, TOPK).astype(jnp.int32)

    def one_device(device_seed):
        perm_key, delta_key, row_key, column_key = jax.random.split(device_seed, 4)
        remaining = jax.random.permutation(perm_key, others).astype(jnp.int32)
        remaining = remaining + (remaining >= hottest).astype(jnp.int32)
        expert_order = jnp.concatenate([hottest[None], remaining])
        shifts = jax.random.randint(delta_key, (pair_count,), 0, spread + 1, dtype=jnp.int32)
        deltas = jnp.stack([shifts, -shifts], axis=1).reshape(2 * pair_count)
        deltas = jnp.concatenate([deltas, jnp.zeros((others - 2 * pair_count,), jnp.int32)])
        counts = baseline + (jnp.arange(others, dtype=jnp.int32) < surplus).astype(jnp.int32) + deltas
        counts = jnp.concatenate([jnp.full((1,), CAP, jnp.int32), counts])
        run_ends = jnp.cumsum(counts).astype(jnp.int32)
        flat_index = jnp.arange(total_picks, dtype=jnp.int32)
        position_of = jnp.sum((flat_index[:, None] >= run_ends[None, :]).astype(jnp.int32), axis=1)
        labels = expert_order[position_of]
        layout_grid = labels.reshape(TOPK, TOK_DEV).T
        layout_grid = layout_grid[jax.random.permutation(row_key, TOK_DEV).astype(jnp.int32)]
        columns = jax.vmap(column_order)(jax.random.split(column_key, TOK_DEV))
        return jnp.take_along_axis(layout_grid, columns, axis=1)
    device_grids = jax.vmap(one_device)(jax.random.split(device_key, TOKENS // TOK_DEV))
    return device_grids.reshape(TOKENS, TOPK).astype(jnp.int32)


def draw_span_len(key, part):
    key = jax.random.fold_in(key, 23)
    length_key, full_key, forced_key = jax.random.split(key, 3)
    lengths = jax.random.randint(length_key, (SEQS,), SEQ_TOK // 2 + 1, SEQ_TOK + 1, dtype=jnp.int32)
    full_mask = jax.random.randint(full_key, (SEQS,), 0, 2, dtype=jnp.int32) == 1
    forced_seq = jax.random.randint(forced_key, (), 0, SEQS, dtype=jnp.int32)
    full_mask = full_mask | (jnp.arange(SEQS, dtype=jnp.int32) == forced_seq)
    return jnp.where(full_mask, SEQ_TOK, lengths).astype(jnp.int32)


def level_of(key, shape, pieces, low, high):
    def one(dim, blocks):
        steps = jax.random.uniform(jax.random.fold_in(jax.random.fold_in(key, 6), dim), (blocks,), jnp.float32, low / len(pieces), high / len(pieces))
        return jnp.repeat(jnp.exp(steps), shape[dim] // blocks).reshape((-1,) + (1,) * (len(shape) - dim - 1))

    factor_of = one(*pieces[0])
    for cut in pieces[1:]:
        factor_of = factor_of * one(*cut)
    return factor_of


def scatter_about(key, extent, deviation, reach, shards=(), kind=jnp.bfloat16):
    level = level_of(key, extent, shards, -0.22, 0.18) if shards else 1.0
    result = jax.random.normal(key, extent, jnp.float32) * deviation * level
    return jnp.minimum(jnp.maximum(result, -reach), reach).astype(kind)


def setup_inputs(seed: int = 0, part: int = 0) -> dict:
    streams_of = jax.random.split(jax.random.key(seed), 9)
    part_splits = jax.random.split(jax.random.fold_in(streams_of[8], part), 9)
    return {
        "hidden": scatter_about(part_splits[0], (TOKENS, D), 1.0, 6.0, ((0, 16),)),
        "norm_gain": jnp.clip(1.0 + 0.18 * jax.random.normal(streams_of[1], (D,), jnp.float32), 0.099609375, 1.8984375).astype(jnp.bfloat16),
        "routes": draw_routes(jax.random.fold_in(jax.random.fold_in(streams_of[8], part), 71), part),
        "gate_vals": jnp.clip(jnp.exp(math.log(0.3) - 2.7080503 * jax.random.uniform(part_splits[3], (TOKENS, TOPK), jnp.float32) ** level_of(part_splits[3], (TOKENS, TOPK), ((0, 16),), -0.2, 0.2)), 0.02, 0.3),
        "span_len": draw_span_len(jax.random.fold_in(jax.random.fold_in(streams_of[8], part), 71), part),
        "w_gate": scatter_about(streams_of[5], (2 * EXPERTS, D, FF_HALF), D ** -0.5, 0.09375, ((0, 16),)),
        "w_up": scatter_about(streams_of[6], (2 * EXPERTS, D, FF_HALF), D ** -0.5, 0.09375, ((0, 16),)),
        "w_down": scatter_about(streams_of[7], (2 * EXPERTS, FF_HALF, D), FF ** -0.5, 0.15625, ((0, 16),)),
    }


def expert_pair(args):
    rows, gate_pair, up_pair, down_pair = args
    parts = []
    for half in range(2):
        gated = jnp.dot(rows, gate_pair[half], preferred_element_type=jnp.float32)
        upper = jnp.dot(rows, up_pair[half], preferred_element_type=jnp.float32)
        act = (jax.nn.silu(gated) * upper).astype(jnp.bfloat16)
        parts.append(jnp.dot(act, down_pair[half], preferred_element_type=jnp.float32).astype(jnp.bfloat16))
    return (parts[0].astype(jnp.float32) + parts[1].astype(jnp.float32)).astype(jnp.bfloat16)

def reference(hidden, norm_gain, routes, gate_vals, span_len, w_gate, w_up, w_down):
    experts = N_EXPERT // 2
    values = hidden.astype(jnp.float32)
    scale = lax.rsqrt(lax.optimization_barrier(jnp.mean(values * values, axis=-1, keepdims=True)) + 1e-06)
    normed = (values * scale * norm_gain.astype(jnp.float32)).astype(jnp.bfloat16)
    position = jnp.arange(TOKENS, dtype=jnp.int32)
    live = position % SEQ_TOK < span_len[(position // SEQ_TOK).astype(jnp.int32)]
    onehot = ((routes[:, :, None] == jnp.arange(experts, dtype=jnp.int32)[None, None, :]) & live[:, None, None]).astype(jnp.int32)
    flat = onehot.reshape(N_EXPERT, TOK_DEV * TOPK, experts)
    rank = jnp.cumsum(flat, axis=1) - flat
    slot = lax.optimization_barrier(jnp.sum(rank * flat, axis=-1)).reshape(TOKENS, TOPK)
    target = routes * CAP + slot
    place = (target[:, :, None] == jnp.arange(experts * CAP, dtype=jnp.int32)[None, None, :]) & live[:, None, None]
    dispatch = jnp.any(place, axis=1).astype(jnp.float32).reshape(N_EXPERT, TOK_DEV, experts * CAP)
    slots = jnp.einsum('stc,std->scd', dispatch, normed.reshape(N_EXPERT, TOK_DEV, D).astype(jnp.float32)).astype(jnp.bfloat16)
    slots = slots.reshape(N_EXPERT, experts, CAP, D).transpose(1, 0, 2, 3).reshape(experts, N_EXPERT * CAP, D)
    results = lax.map(expert_pair, (slots, w_gate.reshape(experts, 2, D, FF_HALF), w_up.reshape(experts, 2, D, FF_HALF), w_down.reshape(experts, 2, FF_HALF, D)))
    results = results.reshape(experts, N_EXPERT, CAP, D).transpose(1, 0, 2, 3).reshape(N_EXPERT, experts * CAP, D)
    weights = lax.optimization_barrier(jnp.sum(jnp.where(place, gate_vals[:, :, None], 0.0), axis=1)).reshape(N_EXPERT, TOK_DEV, experts * CAP)
    moe = jnp.einsum('stc,scd->std', weights, results.astype(jnp.float32), precision=lax.Precision.HIGHEST)
    return (values + moe.reshape(TOKENS, D)).astype(jnp.bfloat16)
```

```python
import jax
import jax.numpy as jnp
from jax import lax
from jax.sharding import PartitionSpec as P

SEQ_TOK = 64


def on_device(hidden, norm_gain, routes, gate_vals, span_len, w_gate, w_up, w_down):
    tok_rows, width = hidden.shape
    count_dev = lax.axis_size("expert")
    experts = count_dev // 2
    my_index = lax.axis_index("expert")
    values = hidden.astype(jnp.float32)
    scale = lax.rsqrt(jnp.mean(values * values, axis=-1, keepdims=True) + 1e-06)
    normed = (values * scale * norm_gain.astype(jnp.float32)).astype(jnp.bfloat16)
    position = my_index * tok_rows + jnp.arange(tok_rows, dtype=jnp.int32)
    seq_match = (position // SEQ_TOK)[:, None] == jnp.arange(span_len.shape[0], dtype=jnp.int32)[
        None, :
    ]
    seq_len = jnp.sum(jnp.where(seq_match, span_len[None, :], 0), axis=-1)
    live = position % SEQ_TOK < seq_len
    chosen = (routes[:, :, None] == jnp.arange(experts, dtype=jnp.int32)[None, None, :]) & live[
        :, None, None
    ]
    weights = jnp.sum(jnp.where(chosen, gate_vals[:, :, None], 0.0), axis=1)
    weights = lax.all_gather(weights, "expert", axis=0, tiled=True)
    mine = jnp.arange(experts, dtype=jnp.int32)[None, :] == my_index // 2
    weight = jnp.sum(jnp.where(mine, weights, 0.0), axis=1, keepdims=True)
    rows = lax.all_gather(normed, "expert", axis=0, tiled=True)
    gated = jnp.dot(rows, w_gate[0], preferred_element_type=jnp.float32)
    upper = jnp.dot(rows, w_up[0], preferred_element_type=jnp.float32)
    act = (jax.nn.silu(gated) * upper).astype(jnp.bfloat16)
    part = jnp.dot(act, w_down[0], preferred_element_type=jnp.float32)
    part = (part * weight).astype(jnp.bfloat16)
    moe = lax.psum_scatter(part, "expert", scatter_dimension=0, tiled=True)
    return (values + moe.astype(jnp.float32)).astype(jnp.bfloat16)


def solution(mesh):
    return jax.shard_map(
        on_device,
        mesh=mesh,
        in_specs=(
            P(("groups", "expert"), None),
            P(),
            P(("groups", "expert"), None),
            P(("groups", "expert"), None),
            P("groups"),
            P("expert", None, None),
            P("expert", None, None),
            P("expert", None, None),
        ),
        out_specs=P(("groups", "expert"), None),
        check_vma=False,
    )
```

```python
import functools

import jax
import jax.numpy as jnp
from jax import lax
from jax.experimental import pallas as pl
from jax.experimental.pallas import tpu as pltpu
from jax.sharding import PartitionSpec as P

SEQ_TOK = 64
EXTRA = 128
VMEM_BUDGET = 60 * 2**20
MESH = pl.DeviceIdType.MESH


def gate_weights(routes, gate_vals, live, lanes):
    columns = lax.broadcasted_iota(jnp.int32, (routes.shape[0], lanes), 1)
    total = jnp.zeros((routes.shape[0], lanes), jnp.float32)
    for k in range(routes.shape[1]):
        total += jnp.where(columns == routes[:, k : k + 1], gate_vals[:, k : k + 1], 0.0)
    return jnp.where(live, total, 0.0)


def normalise(hidden, gain):
    values = hidden.astype(jnp.float32)
    scale = lax.rsqrt(jnp.mean(values * values, axis=-1, keepdims=True) + 1e-06)
    return (values * scale * gain.astype(jnp.float32)).astype(jnp.bfloat16)


def kernel(chips, snake, hidden, gain, routes, gate_vals, span_len, w_gate, w_up, w_down, out,
           x, part, peer_part, arrived, act, wg, wu, wd,
           w_sem, ag_send, ag_recv, agp_send, agp_recv, rs_send, rs_recv, rsp_send, rsp_recv):
    tok, width = hidden.shape
    ff = wg.shape[1]
    half = tok // 2
    far = chips // 2
    me = lax.axis_index("expert")
    chip, core = me // 2, me % 2

    def chip_at(place):
        if not snake:
            return place
        back = place // far
        return 2 * ((1 - back) * place + back * (chips - 1 - place)) + back

    if snake:
        row, deep = chip % 2, chip // 2
        place = (1 - row) * deep + row * (chips - 1 - deep)
    else:
        place = chip
    right = chip_at((place + 1) % chips) * 2 + core
    left = chip_at((place + chips - 1) % chips) * 2 + core
    peer = chip * 2 + 1 - core

    loads = [
        pltpu.make_async_copy(src.at[0], dst, w_sem.at[i])
        for i, (src, dst) in enumerate(((w_gate, wg), (w_up, wu), (w_down, wd)))
    ]
    for load in loads:
        load.start()

    barrier = pltpu.get_barrier_semaphore()
    for other in (left, right, peer):
        pl.semaphore_signal(barrier, inc=1, device_id={"expert": other}, device_id_type=MESH)

    x[0:tok, 0:width] = normalise(hidden[...], gain[...])
    first = me * tok
    offset = first % SEQ_TOK + lax.broadcasted_iota(jnp.int32, (tok, EXTRA // 2), 0)
    live = offset < span_len[first // SEQ_TOK]
    weights = gate_weights(routes[...], gate_vals[...], live, EXTRA // 2)
    upper = weights.astype(jnp.bfloat16)
    lower = (weights - upper.astype(jnp.float32)).astype(jnp.bfloat16)
    x[0:tok, width : width + EXTRA] = jnp.concatenate([upper, lower], axis=1)
    pl.semaphore_wait(barrier, 3)

    last = chips - 1

    def slot(s, d):
        return last if s == far - 1 else 1 + 2 * s + d

    onward = (right, left)
    homeward = (left, right)
    pending = []

    def rows(k, h):
        return pl.ds(2 * tok * k + half * h, half)

    def send_ring(k, s, d, h):
        copy = pltpu.make_async_remote_copy(
            src_ref=x.at[rows(k, h)], dst_ref=x.at[rows(slot(s, d), h)],
            send_sem=ag_send.at[d, s, h], recv_sem=ag_recv.at[d, s, h],
            device_id={"expert": onward[d]}, device_id_type=MESH)
        copy.start()
        pending.append(copy)

    def ring_copy(s, d, h):
        return pltpu.make_async_remote_copy(
            src_ref=x.at[rows(slot(s, d), h)], dst_ref=x.at[rows(slot(s, d), h)],
            send_sem=ag_send.at[d, s, h], recv_sem=ag_recv.at[d, s, h],
            device_id={"expert": onward[d]}, device_id_type=MESH)

    def peer_copy(k, h):
        return pltpu.make_async_remote_copy(
            src_ref=x.at[rows(k, h)], dst_ref=x.at[pl.ds(2 * tok * k + tok + half * h, half)],
            send_sem=agp_send.at[k, h], recv_sem=agp_recv.at[k, h],
            device_id={"expert": peer}, device_id_type=MESH)

    def send_peer(k, h):
        copy = peer_copy(k, h)
        copy.start()
        pending.append(copy)

    def part_copy(k):
        return pltpu.make_async_remote_copy(
            src_ref=part.at[pl.ds(2 * tok * k + tok, tok)], dst_ref=peer_part.at[pl.ds(tok * k, tok)],
            send_sem=rsp_send.at[k], recv_sem=rsp_recv.at[k],
            device_id={"expert": peer}, device_id_type=MESH)

    def compute(start, count):
        block = pl.ds(start, count)
        marks = x[block, width : width + EXTRA].astype(jnp.float32)
        lane = lax.broadcasted_iota(jnp.int32, marks.shape, 1) % (EXTRA // 2)
        weight = jnp.sum(jnp.where(lane == chip, marks, 0.0), axis=1, keepdims=True)
        tile = min(256, ff)

        @pl.loop(0, ff // tile)
        def _(j):
            cols = pl.ds(pl.multiple_of(j * tile, tile), tile)
            rows_in = x[block, 0:width]
            gated = jnp.dot(rows_in, wg[:, cols], preferred_element_type=jnp.float32)
            upped = jnp.dot(rows_in, wu[:, cols], preferred_element_type=jnp.float32)
            act[0:count, cols] = (gated / (1.0 + jnp.exp(-gated)) * upped).astype(jnp.bfloat16)

        wide = min(512, width)

        @pl.loop(0, width // wide)
        def _(j):
            cols = pl.ds(pl.multiple_of(j * wide, wide), wide)
            product = jnp.dot(act[0:count, :], wd[:, cols], preferred_element_type=jnp.float32)
            part[block, cols] = (product * weight).astype(jnp.bfloat16)

        for k in range(start // (2 * tok), (start + count) // (2 * tok)):
            copy = part_copy(k)
            copy.start()
            pending.append(copy)

    for h in range(2):
        for d in range(2):
            send_ring(0, 0, d, h)
        send_peer(0, h)
    for load in loads:
        load.wait()
    for h in range(2):
        peer_copy(0, h).wait_recv()
    compute(0, 2 * tok)

    for s in range(far):
        for h in range(2):
            for d in range(2):
                if s == far - 1 and h != d:
                    continue
                k = slot(s, d)
                ring_copy(s, d, h).wait_recv()
                if s + 1 < far - 1 or (s + 1 == far - 1 and h == d):
                    send_ring(k, s + 1, d, h)
                send_peer(k, h)
        for k in sorted({slot(s, 0), slot(s, 1)}):
            for h in range(2):
                peer_copy(k, h).wait_recv()
        if s < far - 1:
            compute(2 * tok * slot(s, 0), 4 * tok)
        else:
            compute(2 * tok * last, 2 * tok)

    def place_of(s, d, h):
        k = slot(s, d) if s >= 0 else (last if d else 0)
        return arrived.at[pl.ds(tok * k + half * h, half)]

    def sum_copy(s, d, h):
        return pltpu.make_async_remote_copy(
            src_ref=part.at[rows(slot(s, d), h)], dst_ref=place_of(s - 1, d, h),
            send_sem=rs_send.at[d, s, h], recv_sem=rs_recv.at[d, s, h],
            device_id={"expert": homeward[d]}, device_id_type=MESH)

    def local_sum(k, h):
        mine = part[rows(k, h), :].astype(jnp.float32)
        return mine + peer_part[pl.ds(tok * k + half * h, half), :].astype(jnp.float32)

    def send_sum(s, d, h):
        k = slot(s, d)
        total = local_sum(k, h)
        if s < far - 2 or (s == far - 2 and h == d):
            sum_copy(s + 1, d, h).wait_recv()
            total += place_of(s, d, h)[...].astype(jnp.float32)
        part[rows(k, h), :] = total.astype(jnp.bfloat16)
        copy = sum_copy(s, d, h)
        copy.start()
        pending.append(copy)

    for d in range(2):
        part_copy(slot(far - 2, d)).wait_recv()
        send_sum(far - 2, d, 1 - d)
    part_copy(last).wait_recv()
    for d in range(2):
        send_sum(far - 1, d, d)
    for d in range(2):
        send_sum(far - 2, d, d)
    for s in range(far - 3, -1, -1):
        for d in range(2):
            part_copy(slot(s, d)).wait_recv()
        for flip in (1, 0):
            for d in range(2):
                send_sum(s, d, d ^ flip)
    part_copy(0).wait_recv()
    for h in range(2):
        for d in range(2):
            sum_copy(0, d, h).wait_recv()
        total = local_sum(0, h)
        for d in range(2):
            total += place_of(-1, d, h)[...].astype(jnp.float32)
        here = slice(half * h, half * (h + 1))
        out[here, :] = (hidden[here, :].astype(jnp.float32) + total).astype(out.dtype)
    for copy in pending:
        copy.wait_send()


def vmem_need(tok, width, ff, chips):
    gathered = 2 * chips * tok
    return 2 * (gathered * (3 * width + EXTRA) + 3 * width * ff + 16 * tok * width)


def fused(snake, hidden, norm_gain, routes, gate_vals, span_len, w_gate, w_up, w_down):
    tok, width = hidden.shape
    ff = w_gate.shape[2]
    chips = lax.axis_size("expert") // 2
    far = chips // 2
    dma = pltpu.SemaphoreType.DMA
    in_vmem = pl.BlockSpec(memory_space=pltpu.VMEM)
    in_hbm = pl.BlockSpec(memory_space=pl.ANY)
    flops = 2 * 3 * 2 * chips * tok * width * ff
    return pl.pallas_call(
        functools.partial(kernel, chips, snake),
        out_shape=jax.ShapeDtypeStruct((tok, width), hidden.dtype),
        in_specs=[in_vmem] * 4 + [pl.BlockSpec(memory_space=pltpu.SMEM)] + [in_hbm] * 3,
        out_specs=in_vmem,
        scratch_shapes=[
            pltpu.VMEM((2 * chips * tok, width + EXTRA), jnp.bfloat16),
            pltpu.VMEM((2 * chips * tok, width), jnp.bfloat16),
            pltpu.VMEM((chips * tok, width), jnp.bfloat16),
            pltpu.VMEM((chips * tok, width), jnp.bfloat16),
            pltpu.VMEM((4 * tok, ff), jnp.bfloat16),
            pltpu.VMEM((width, ff), jnp.bfloat16),
            pltpu.VMEM((width, ff), jnp.bfloat16),
            pltpu.VMEM((ff, width), jnp.bfloat16),
            dma((3,)),
            dma((2, far, 2)), dma((2, far, 2)), dma((chips, 2)), dma((chips, 2)),
            dma((2, far, 2)), dma((2, far, 2)), dma((chips,)), dma((chips,)),
        ],
        compiler_params=pltpu.CompilerParams(
            collective_id=0, has_side_effects=True, vmem_limit_bytes=VMEM_BUDGET
        ),
        cost_estimate=pl.CostEstimate(
            flops=flops, bytes_accessed=6 * width * ff, transcendentals=2 * chips * tok * ff
        ),
    )(hidden, norm_gain.reshape(1, width), routes, gate_vals, span_len, w_gate, w_up, w_down)


def with_collectives(hidden, norm_gain, routes, gate_vals, span_len, w_gate, w_up, w_down):
    tok = hidden.shape[0]
    experts = lax.axis_size("expert") // 2
    me = lax.axis_index("expert")
    position = me * tok + jnp.arange(tok, dtype=jnp.int32)
    live = position % SEQ_TOK < span_len[position // SEQ_TOK]
    weights = gate_weights(routes, gate_vals, live[:, None], experts)
    weights = lax.all_gather(weights, "expert", axis=0, tiled=True)
    mine = jnp.arange(experts, dtype=jnp.int32)[None, :] == me // 2
    weight = jnp.sum(jnp.where(mine, weights, 0.0), axis=1, keepdims=True)
    rows = lax.all_gather(normalise(hidden, norm_gain), "expert", axis=0, tiled=True)
    gated = jnp.dot(rows, w_gate[0], preferred_element_type=jnp.float32)
    upper = jnp.dot(rows, w_up[0], preferred_element_type=jnp.float32)
    act = (jax.nn.silu(gated) * upper).astype(jnp.bfloat16)
    part = jnp.dot(act, w_down[0], preferred_element_type=jnp.float32)
    part = (part * weight).astype(jnp.bfloat16)
    moe = lax.psum_scatter(part, "expert", scatter_dimension=0, tiled=True)
    return (hidden.astype(jnp.float32) + moe.astype(jnp.float32)).astype(jnp.bfloat16)


def solution(mesh):
    devices = mesh.shape["expert"]

    def on_device(hidden, *rest):
        tok, width = hidden.shape
        fits = vmem_need(tok, width, rest[-1].shape[1], devices // 2) <= VMEM_BUDGET - 2**23
        if fits and devices % 4 == 0 and devices >= 12 and SEQ_TOK % tok == 0 and tok % 32 == 0:
            return fused(devices == 16, hidden, *rest)
        return with_collectives(hidden, *rest)

    return jax.shard_map(
        on_device,
        mesh=mesh,
        in_specs=(
            P(("groups", "expert"), None),
            P(),
            P(("groups", "expert"), None),
            P(("groups", "expert"), None),
            P("groups"),
            P("expert", None, None),
            P("expert", None, None),
            P("expert", None, None),
        ),
        out_specs=P(("groups", "expert"), None),
        check_vma=False,
    )
```

```python
import functools

import jax
import jax.numpy as jnp
from jax import lax
from jax.experimental import pallas as pl
from jax.experimental.pallas import tpu as pltpu
from jax.sharding import PartitionSpec as P

SEQ_TOK = 64
EXTRA = 128
VMEM_BUDGET = 60 * 2**20
MESH = pl.DeviceIdType.MESH


def gate_weights(routes, gate_vals, live, lanes):
    named = lax.broadcasted_iota(jnp.int32, (lanes, routes.shape[1]), 0)
    total = jnp.zeros((lanes, routes.shape[1]), jnp.float32)
    for k in range(routes.shape[0]):
        total += jnp.where(named == routes[k : k + 1, :], gate_vals[k : k + 1, :], 0.0)
    return jnp.where(live, total, 0.0)


def normalise(hidden, gain):
    values = hidden.astype(jnp.float32)
    scale = lax.rsqrt(jnp.mean(values * values, axis=-1, keepdims=True) + 1e-06)
    return (values * scale * gain.astype(jnp.float32)[None, :]).astype(jnp.bfloat16)


def kernel(chips, snake, hidden, gain, routes, gate_vals, span_len, w_gate, w_up, w_down, out,
           x, part, peer_part, arrived, act, wg, wu, wd,
           w_sem, ag_send, ag_recv, agp_send, agp_recv, rs_send, rs_recv, rsp_send, rsp_recv):
    tok, width = hidden.shape
    ff = wg.shape[1]
    half = tok // 2
    far = chips // 2
    me = lax.axis_index("expert")
    chip, core = me // 2, me % 2

    def chip_at(place):
        if not snake:
            return place
        back = place // far
        return 2 * ((1 - back) * place + back * (chips - 1 - place)) + back

    if snake:
        row, deep = chip % 2, chip // 2
        place = (1 - row) * deep + row * (chips - 1 - deep)
    else:
        place = chip
    right = chip_at((place + 1) % chips) * 2 + core
    left = chip_at((place + chips - 1) % chips) * 2 + core
    peer = chip * 2 + 1 - core

    loads = [
        pltpu.make_async_copy(src.at[0], dst, w_sem.at[i])
        for i, (src, dst) in enumerate(((w_gate, wg), (w_up, wu), (w_down, wd)))
    ]
    for load in loads:
        load.start()

    barrier = pltpu.get_barrier_semaphore()
    for other in (left, right, peer):
        pl.semaphore_signal(barrier, inc=1, device_id={"expert": other}, device_id_type=MESH)

    first = me * tok
    offset = first % SEQ_TOK + lax.broadcasted_iota(jnp.int32, (EXTRA // 2, tok), 1)
    live = offset < span_len[first // SEQ_TOK]
    weights = gate_weights(routes[...], gate_vals[...], live, EXTRA // 2)
    upper = weights.astype(jnp.bfloat16)
    lower = (weights - upper.astype(jnp.float32)).astype(jnp.bfloat16)
    same = lax.broadcasted_iota(jnp.int32, (tok, tok), 0) == lax.broadcasted_iota(
        jnp.int32, (tok, tok), 1
    )
    x[0:tok, width : width + EXTRA] = lax.dot_general(
        same.astype(jnp.bfloat16), jnp.concatenate([upper, lower], axis=0),
        (((1,), (1,)), ((), ())), preferred_element_type=jnp.float32,
    ).astype(jnp.bfloat16)

    last = chips - 1
    onward = (right, left)
    homeward = (left, right)
    pending = []

    def base(s, d, h, own):
        if s < 0:
            return (1 - own) * tok + h * half
        if s == far - 1:
            return 2 * tok * last + (1 - own) * tok + h * half
        return 2 * tok * (1 + 2 * s + (h ^ d)) + d * tok + (1 - own) * half

    def slot(s, d):
        return 0 if s < 0 else last if s == far - 1 else 1 + 2 * s + d

    def rows(s, d, h, own=1):
        return pl.ds(base(s, d, h, own), half)

    def begin(copy):
        copy.start()
        pending.append(copy)

    def ring_copy(s, d, h, source=None):
        return pltpu.make_async_remote_copy(
            src_ref=x.at[rows(s if source is None else source, d, h)], dst_ref=x.at[rows(s, d, h)],
            send_sem=ag_send.at[d, s, h], recv_sem=ag_recv.at[d, s, h],
            device_id={"expert": onward[d]}, device_id_type=MESH)

    def peer_copy(s, d, h):
        return pltpu.make_async_remote_copy(
            src_ref=x.at[rows(s, d, h)], dst_ref=x.at[rows(s, d, h, 0)],
            send_sem=agp_send.at[slot(s, d), h], recv_sem=agp_recv.at[slot(s, d), h],
            device_id={"expert": peer}, device_id_type=MESH)

    def held(s, d, h):
        return pl.ds(tok * slot(s, d) + half * h, half)

    def part_copy(s, d, h):
        return pltpu.make_async_remote_copy(
            src_ref=part.at[rows(s, d, h, 0)], dst_ref=peer_part.at[held(s, d, h)],
            send_sem=rsp_send.at[slot(s, d), h], recv_sem=rsp_recv.at[slot(s, d), h],
            device_id={"expert": peer}, device_id_type=MESH)

    def chunks(b):
        if b == 0:
            return [(-1, 0, 0), (-1, 0, 1)]
        if b == last:
            return [(far - 1, 0, 0), (far - 1, 1, 1)]
        s, f = (b - 1) // 2, (b - 1) % 2
        return [(s, 0, f), (s, 1, 1 - f)]

    def forward(b):
        for s, d, h in chunks(b):
            ring_copy(s, d, h).wait_recv()
            if s + 1 < far - 1 or (s + 1 == far - 1 and h == d):
                begin(ring_copy(s + 1, d, h, s))
            begin(peer_copy(s, d, h))

    def compute(b):
        for chunk in chunks(b):
            peer_copy(*chunk).wait_recv()
        count = 2 * tok
        block = pl.ds(count * b, count)
        marks = x[block, width : width + EXTRA].astype(jnp.float32)
        lane = lax.broadcasted_iota(jnp.int32, marks.shape, 1) % (EXTRA // 2)
        weight = jnp.sum(jnp.where(lane == chip, marks, 0.0), axis=1, keepdims=True)
        tile = min(256, ff)

        @pl.loop(0, ff // tile)
        def _(j):
            cols = pl.ds(pl.multiple_of(j * tile, tile), tile)
            rows_in = x[block, 0:width]
            gated = jnp.dot(rows_in, wg[:, cols], preferred_element_type=jnp.float32)
            upped = jnp.dot(rows_in, wu[:, cols], preferred_element_type=jnp.float32)
            act[:, cols] = (gated / (1.0 + jnp.exp(-gated)) * upped).astype(jnp.bfloat16)

        wide = min(512, width)

        @pl.loop(0, width // wide)
        def _(j):
            cols = pl.ds(pl.multiple_of(j * wide, wide), wide)
            product = jnp.dot(act[...], wd[:, cols], preferred_element_type=jnp.float32)
            part[block, cols] = (product * weight).astype(jnp.bfloat16)

        for chunk in chunks(b):
            begin(part_copy(*chunk))

    for h in range(2):
        here = slice(half * h, half * (h + 1))
        x[here, 0:width] = normalise(hidden[here, :], gain[...])
        if h == 0:
            pl.semaphore_wait(barrier, 3)
        begin(ring_copy(0, h, h, -1))
    for h in range(2):
        begin(ring_copy(0, 1 - h, h, -1))
        begin(peer_copy(-1, 0, h))
    forward(1)
    for load in loads:
        load.wait()
    for b in range(last - 1):
        compute(b)
        forward(b + 2)

    def place_of(s, d, h):
        return arrived.at[held(far - 1 if s < 0 and d else s, d, h)]

    def sum_copy(s, d, h):
        return pltpu.make_async_remote_copy(
            src_ref=part.at[rows(s, d, h)], dst_ref=place_of(s - 1, d, h),
            send_sem=rs_send.at[d, s, h], recv_sem=rs_recv.at[d, s, h],
            device_id={"expert": homeward[d]}, device_id_type=MESH)

    def local_sum(s, d, h):
        part_copy(s, d, h).wait_recv()
        mine = part[rows(s, d, h), :].astype(jnp.float32)
        return mine + peer_part[held(s, d, h), :].astype(jnp.float32)

    def send_sum(s, d, h):
        total = local_sum(s, d, h)
        if s < far - 2 or (s == far - 2 and h == d):
            sum_copy(s + 1, d, h).wait_recv()
            total += place_of(s, d, h)[...].astype(jnp.float32)
        part[rows(s, d, h), :] = total.astype(jnp.bfloat16)
        begin(sum_copy(s, d, h))

    compute(last - 1)
    for d in range(2):
        send_sum(far - 2, d, 1 - d)
    compute(last)
    for d in range(2):
        send_sum(far - 1, d, d)
    for d in range(2):
        send_sum(far - 2, d, d)
    for s in range(far - 3, -1, -1):
        for flip in (1, 0):
            for d in range(2):
                send_sum(s, d, d ^ flip)
    for h in (1, 0):
        total = local_sum(-1, 0, h)
        for d in range(2):
            sum_copy(0, d, h).wait_recv()
            total += place_of(-1, d, h)[...].astype(jnp.float32)
        here = slice(half * h, half * (h + 1))
        out[here, :] = (hidden[here, :].astype(jnp.float32) + total).astype(out.dtype)
    for copy in pending:
        copy.wait_send()


def vmem_need(tok, width, ff, chips):
    gathered = 2 * chips * tok
    return 2 * (gathered * (3 * width + EXTRA) + 3 * width * ff + 16 * tok * width)


def fused(snake, hidden, norm_gain, routes, gate_vals, span_len, w_gate, w_up, w_down):
    tok, width = hidden.shape
    ff = w_gate.shape[2]
    chips = lax.axis_size("expert") // 2
    far = chips // 2
    dma = pltpu.SemaphoreType.DMA
    in_vmem = pl.BlockSpec(memory_space=pltpu.VMEM)
    in_hbm = pl.BlockSpec(memory_space=pl.ANY)
    flops = 2 * 3 * 2 * chips * tok * width * ff
    return pl.pallas_call(
        functools.partial(kernel, chips, snake),
        out_shape=jax.ShapeDtypeStruct((tok, width), hidden.dtype),
        in_specs=[in_vmem] * 4 + [pl.BlockSpec(memory_space=pltpu.SMEM)] + [in_hbm] * 3,
        out_specs=in_vmem,
        scratch_shapes=[
            pltpu.VMEM((2 * chips * tok, width + EXTRA), jnp.bfloat16),
            pltpu.VMEM((2 * chips * tok, width), jnp.bfloat16),
            pltpu.VMEM((chips * tok, width), jnp.bfloat16),
            pltpu.VMEM((chips * tok, width), jnp.bfloat16),
            pltpu.VMEM((2 * tok, ff), jnp.bfloat16),
            pltpu.VMEM((width, ff), jnp.bfloat16),
            pltpu.VMEM((width, ff), jnp.bfloat16),
            pltpu.VMEM((ff, width), jnp.bfloat16),
            dma((3,)),
            dma((2, far, 2)), dma((2, far, 2)), dma((chips, 2)), dma((chips, 2)),
            dma((2, far, 2)), dma((2, far, 2)), dma((chips, 2)), dma((chips, 2)),
        ],
        compiler_params=pltpu.CompilerParams(
            collective_id=0, has_side_effects=True, vmem_limit_bytes=VMEM_BUDGET
        ),
        cost_estimate=pl.CostEstimate(
            flops=flops, bytes_accessed=6 * width * ff, transcendentals=2 * chips * tok * ff
        ),
    )(hidden, norm_gain, routes.T, gate_vals.T, span_len, w_gate, w_up, w_down)


def with_collectives(hidden, norm_gain, routes, gate_vals, span_len, w_gate, w_up, w_down):
    tok = hidden.shape[0]
    experts = lax.axis_size("expert") // 2
    me = lax.axis_index("expert")
    position = me * tok + jnp.arange(tok, dtype=jnp.int32)
    live = position % SEQ_TOK < span_len[position // SEQ_TOK]
    weights = gate_weights(routes.T, gate_vals.T, live[None, :], experts).T
    weights = lax.all_gather(weights, "expert", axis=0, tiled=True)
    mine = jnp.arange(experts, dtype=jnp.int32)[None, :] == me // 2
    weight = jnp.sum(jnp.where(mine, weights, 0.0), axis=1, keepdims=True)
    rows = lax.all_gather(normalise(hidden, norm_gain), "expert", axis=0, tiled=True)
    gated = jnp.dot(rows, w_gate[0], preferred_element_type=jnp.float32)
    upper = jnp.dot(rows, w_up[0], preferred_element_type=jnp.float32)
    act = (jax.nn.silu(gated) * upper).astype(jnp.bfloat16)
    part = jnp.dot(act, w_down[0], preferred_element_type=jnp.float32)
    part = (part * weight).astype(jnp.bfloat16)
    moe = lax.psum_scatter(part, "expert", scatter_dimension=0, tiled=True)
    return (hidden.astype(jnp.float32) + moe.astype(jnp.float32)).astype(jnp.bfloat16)


def solution(mesh):
    devices = mesh.shape["expert"]

    def on_device(hidden, *rest):
        tok, width = hidden.shape
        fits = vmem_need(tok, width, rest[-1].shape[1], devices // 2) <= VMEM_BUDGET - 2**23
        if fits and devices % 4 == 0 and devices >= 12 and SEQ_TOK % tok == 0 and tok % 32 == 0:
            return fused(devices == 16, hidden, *rest)
        return with_collectives(hidden, *rest)

    return jax.shard_map(
        on_device,
        mesh=mesh,
        in_specs=(
            P(("groups", "expert"), None),
            P(),
            P(("groups", "expert"), None),
            P(("groups", "expert"), None),
            P("groups"),
            P("expert", None, None),
            P("expert", None, None),
            P("expert", None, None),
        ),
        out_specs=P(("groups", "expert"), None),
        check_vma=False,
    )
```

```python
import functools

import jax
import jax.numpy as jnp
from jax import lax
from jax.experimental import pallas as pl
from jax.experimental.pallas import tpu as pltpu
from jax.sharding import PartitionSpec as P

SEQ_TOK = 64
EXTRA = 128
VMEM_BUDGET = 60 * 2**20
MESH = pl.DeviceIdType.MESH


def gate_weights(routes, gate_vals, live, lanes):
    named = lax.broadcasted_iota(jnp.int32, (lanes, routes.shape[1]), 0)
    total = jnp.zeros((lanes, routes.shape[1]), jnp.float32)
    for k in range(routes.shape[0]):
        total += jnp.where(named == routes[k : k + 1, :], gate_vals[k : k + 1, :], 0.0)
    return jnp.where(live, total, 0.0)


def normalise(hidden, gain):
    values = hidden.astype(jnp.float32)
    scale = lax.rsqrt(jnp.mean(values * values, axis=-1, keepdims=True) + 1e-06)
    return (values * scale * gain.astype(jnp.float32)[None, :]).astype(jnp.bfloat16)


def kernel(chips, snake, hidden, gain, routes, gate_vals, span_len, w_gate, w_up, w_down, out,
           x, part, peer_part, arrived, act, wg, wu, wd,
           w_sem, ag_send, ag_recv, agp_send, agp_recv, rs_send, rs_recv, rsp_send, rsp_recv):
    tok, width = hidden.shape
    ff = wg.shape[1]
    half = tok // 2
    far = chips // 2
    me = lax.axis_index("expert")
    chip, core = me // 2, me % 2

    def chip_at(place):
        if not snake:
            return place
        back = place // far
        return 2 * ((1 - back) * place + back * (chips - 1 - place)) + back

    if snake:
        row, deep = chip % 2, chip // 2
        place = (1 - row) * deep + row * (chips - 1 - deep)
    else:
        place = chip
    right = chip_at((place + 1) % chips) * 2 + core
    left = chip_at((place + chips - 1) % chips) * 2 + core
    peer = chip * 2 + 1 - core

    loads = [
        pltpu.make_async_copy(src.at[0], dst, w_sem.at[i])
        for i, (src, dst) in enumerate(((w_gate, wg), (w_up, wu), (w_down, wd)))
    ]
    for load in loads:
        load.start()

    barrier = pltpu.get_barrier_semaphore()
    for other in (left, right, peer):
        pl.semaphore_signal(barrier, inc=1, device_id={"expert": other}, device_id_type=MESH)

    first = me * tok
    offset = first % SEQ_TOK + lax.broadcasted_iota(jnp.int32, (EXTRA // 2, tok), 1)
    live = offset < span_len[first // SEQ_TOK]
    weights = gate_weights(routes[...], gate_vals[...], live, EXTRA // 2)
    upper = weights.astype(jnp.bfloat16)
    lower = (weights - upper.astype(jnp.float32)).astype(jnp.bfloat16)
    same = lax.broadcasted_iota(jnp.int32, (tok, tok), 0) == lax.broadcasted_iota(
        jnp.int32, (tok, tok), 1
    )
    x[0:tok, width : width + EXTRA] = lax.dot_general(
        same.astype(jnp.bfloat16), jnp.concatenate([upper, lower], axis=0),
        (((1,), (1,)), ((), ())), preferred_element_type=jnp.float32,
    ).astype(jnp.bfloat16)

    last = chips - 1
    onward = (right, left)
    homeward = (left, right)
    pending = []

    def base(s, d, h, own):
        if s < 0:
            return (1 - own) * tok + h * half
        if s == far - 1:
            return 2 * tok * last + (1 - own) * tok + h * half
        return 2 * tok * (1 + 2 * s + (h ^ d)) + d * tok + (1 - own) * half

    def slot(s, d):
        return 0 if s < 0 else last if s == far - 1 else 1 + 2 * s + d

    def rows(s, d, h, own=1):
        return pl.ds(base(s, d, h, own), half)

    def begin(copy):
        copy.start()
        pending.append(copy)

    def ring_copy(s, d, h, source=None):
        return pltpu.make_async_remote_copy(
            src_ref=x.at[rows(s if source is None else source, d, h)], dst_ref=x.at[rows(s, d, h)],
            send_sem=ag_send.at[d, s, h], recv_sem=ag_recv.at[d, s, h],
            device_id={"expert": onward[d]}, device_id_type=MESH)

    def peer_copy(s, d, h):
        return pltpu.make_async_remote_copy(
            src_ref=x.at[rows(s, d, h)], dst_ref=x.at[rows(s, d, h, 0)],
            send_sem=agp_send.at[slot(s, d), h], recv_sem=agp_recv.at[slot(s, d), h],
            device_id={"expert": peer}, device_id_type=MESH)

    def held(s, d, h):
        return pl.ds(tok * slot(s, d) + half * h, half)

    def part_copy(s, d, h):
        return pltpu.make_async_remote_copy(
            src_ref=part.at[rows(s, d, h, 0)], dst_ref=peer_part.at[held(s, d, h)],
            send_sem=rsp_send.at[slot(s, d), h], recv_sem=rsp_recv.at[slot(s, d), h],
            device_id={"expert": peer}, device_id_type=MESH)

    def chunks(b):
        if b == 0:
            return [(-1, 0, 0), (-1, 0, 1)]
        if b == last:
            return [(far - 1, 0, 0), (far - 1, 1, 1)]
        s, f = (b - 1) // 2, (b - 1) % 2
        return [(s, 0, f), (s, 1, 1 - f)]

    def forward(b):
        for s, d, h in chunks(b):
            ring_copy(s, d, h).wait_recv()
            if s + 1 < far - 1 or (s + 1 == far - 1 and h == d):
                begin(ring_copy(s + 1, d, h, s))
            begin(peer_copy(s, d, h))

    def compute(b):
        for chunk in chunks(b):
            peer_copy(*chunk).wait_recv()
        count = 2 * tok
        block = pl.ds(count * b, count)
        marks = x[block, width : width + EXTRA].astype(jnp.float32)
        lane = lax.broadcasted_iota(jnp.int32, marks.shape, 1) % (EXTRA // 2)
        weight = jnp.sum(jnp.where(lane == chip, marks, 0.0), axis=1, keepdims=True)
        tile = min(256, ff)

        @pl.loop(0, ff // tile)
        def _(j):
            cols = pl.ds(pl.multiple_of(j * tile, tile), tile)
            rows_in = x[block, 0:width]
            gated = jnp.dot(rows_in, wg[:, cols], preferred_element_type=jnp.float32)
            upped = jnp.dot(rows_in, wu[:, cols], preferred_element_type=jnp.float32)
            act[:, cols] = (gated / (1.0 + jnp.exp(-gated)) * upped).astype(jnp.bfloat16)

        wide = min(1024, width)

        @pl.loop(0, width // wide)
        def _(j):
            cols = pl.ds(pl.multiple_of(j * wide, wide), wide)
            product = jnp.dot(act[...], wd[:, cols], preferred_element_type=jnp.float32)
            part[block, cols] = (product * weight).astype(jnp.bfloat16)

        for chunk in chunks(b):
            begin(part_copy(*chunk))

    for h in range(2):
        here = slice(half * h, half * (h + 1))
        x[here, 0:width] = normalise(hidden[here, :], gain[...])
        if h == 0:
            pl.semaphore_wait(barrier, 3)
        begin(ring_copy(0, h, h, -1))
    for h in range(2):
        begin(ring_copy(0, 1 - h, h, -1))
        begin(peer_copy(-1, 0, h))
    forward(1)
    for load in loads:
        load.wait()
    compute(0)
    for b in range(1, last):
        compute(b)
        if b + 1 < last:
            forward(b + 1)

    def pieces(d, h):
        return ((0, half // 2, h), (half // 2, half // 2, 2)) if h == d else ((0, half, h),)

    def cut(block, piece):
        return pl.ds(block.start + piece[0], piece[1])

    def home(s, d, h):
        return held(far - 1 if s < 0 and d else s, d, h)

    def sum_copy(s, d, h, piece):
        return pltpu.make_async_remote_copy(
            src_ref=part.at[cut(rows(s, d, h), piece)],
            dst_ref=arrived.at[cut(home(s - 1, d, h), piece)],
            send_sem=rs_send.at[d, s, piece[2]], recv_sem=rs_recv.at[d, s, piece[2]],
            device_id={"expert": homeward[d]}, device_id_type=MESH)

    def send_sum(s, d, h):
        part_copy(s, d, h).wait_recv()
        for piece in pieces(d, h):
            mine = cut(rows(s, d, h), piece)
            total = part[mine, :].astype(jnp.float32)
            total += peer_part[cut(held(s, d, h), piece), :].astype(jnp.float32)
            if s < far - 2 or (s == far - 2 and h == d):
                sum_copy(s + 1, d, h, piece).wait_recv()
                total += arrived[cut(home(s, d, h), piece), :].astype(jnp.float32)
            part[mine, :] = total.astype(jnp.bfloat16)
            begin(sum_copy(s, d, h, piece))

    for d in range(2):
        send_sum(far - 2, d, 1 - d)
    forward(last)
    compute(last)
    for d in range(2):
        send_sum(far - 1, d, d)
    for d in range(2):
        send_sum(far - 2, d, d)
    for s in range(far - 3, -1, -1):
        for flip in (1, 0):
            for d in range(2):
                send_sum(s, d, d ^ flip)
    for h in (1, 0):
        part_copy(-1, 0, h).wait_recv()
        total = part[rows(-1, 0, h), :].astype(jnp.float32)
        total += peer_part[held(-1, 0, h), :].astype(jnp.float32)
        for d in range(2):
            for piece in pieces(d, h):
                sum_copy(0, d, h, piece).wait_recv()
            total += arrived[home(-1, d, h), :].astype(jnp.float32)
        here = slice(half * h, half * (h + 1))
        out[here, :] = (hidden[here, :].astype(jnp.float32) + total).astype(out.dtype)
    for copy in pending:
        copy.wait_send()


def vmem_need(tok, width, ff, chips):
    gathered = 2 * chips * tok
    return 2 * (gathered * (3 * width + EXTRA) + 3 * width * ff + 16 * tok * width)


def fused(snake, hidden, norm_gain, routes, gate_vals, span_len, w_gate, w_up, w_down):
    tok, width = hidden.shape
    ff = w_gate.shape[2]
    chips = lax.axis_size("expert") // 2
    far = chips // 2
    dma = pltpu.SemaphoreType.DMA
    in_vmem = pl.BlockSpec(memory_space=pltpu.VMEM)
    in_hbm = pl.BlockSpec(memory_space=pl.ANY)
    flops = 2 * 3 * 2 * chips * tok * width * ff
    return pl.pallas_call(
        functools.partial(kernel, chips, snake),
        out_shape=jax.ShapeDtypeStruct((tok, width), hidden.dtype),
        in_specs=[in_vmem] * 4 + [pl.BlockSpec(memory_space=pltpu.SMEM)] + [in_hbm] * 3,
        out_specs=in_vmem,
        scratch_shapes=[
            pltpu.VMEM((2 * chips * tok, width + EXTRA), jnp.bfloat16),
            pltpu.VMEM((2 * chips * tok, width), jnp.bfloat16),
            pltpu.VMEM((chips * tok, width), jnp.bfloat16),
            pltpu.VMEM((chips * tok, width), jnp.bfloat16),
            pltpu.VMEM((2 * tok, ff), jnp.bfloat16),
            pltpu.VMEM((width, ff), jnp.bfloat16),
            pltpu.VMEM((width, ff), jnp.bfloat16),
            pltpu.VMEM((ff, width), jnp.bfloat16),
            dma((3,)),
            dma((2, far, 2)), dma((2, far, 2)), dma((chips, 2)), dma((chips, 2)),
            dma((2, far, 3)), dma((2, far, 3)), dma((chips, 2)), dma((chips, 2)),
        ],
        compiler_params=pltpu.CompilerParams(
            collective_id=0, has_side_effects=True, vmem_limit_bytes=VMEM_BUDGET
        ),
        cost_estimate=pl.CostEstimate(
            flops=flops, bytes_accessed=6 * width * ff, transcendentals=2 * chips * tok * ff
        ),
    )(hidden, norm_gain, routes.T, gate_vals.T, span_len, w_gate, w_up, w_down)


def with_collectives(hidden, norm_gain, routes, gate_vals, span_len, w_gate, w_up, w_down):
    tok = hidden.shape[0]
    experts = lax.axis_size("expert") // 2
    me = lax.axis_index("expert")
    position = me * tok + jnp.arange(tok, dtype=jnp.int32)
    live = position % SEQ_TOK < span_len[position // SEQ_TOK]
    weights = gate_weights(routes.T, gate_vals.T, live[None, :], experts).T
    weights = lax.all_gather(weights, "expert", axis=0, tiled=True)
    mine = jnp.arange(experts, dtype=jnp.int32)[None, :] == me // 2
    weight = jnp.sum(jnp.where(mine, weights, 0.0), axis=1, keepdims=True)
    rows = lax.all_gather(normalise(hidden, norm_gain), "expert", axis=0, tiled=True)
    gated = jnp.dot(rows, w_gate[0], preferred_element_type=jnp.float32)
    upper = jnp.dot(rows, w_up[0], preferred_element_type=jnp.float32)
    act = (jax.nn.silu(gated) * upper).astype(jnp.bfloat16)
    part = jnp.dot(act, w_down[0], preferred_element_type=jnp.float32)
    part = (part * weight).astype(jnp.bfloat16)
    moe = lax.psum_scatter(part, "expert", scatter_dimension=0, tiled=True)
    return (hidden.astype(jnp.float32) + moe.astype(jnp.float32)).astype(jnp.bfloat16)


def solution(mesh):
    devices = mesh.shape["expert"]

    def on_device(hidden, *rest):
        tok, width = hidden.shape
        fits = vmem_need(tok, width, rest[-1].shape[1], devices // 2) <= VMEM_BUDGET - 2**23
        if fits and devices % 4 == 0 and devices >= 12 and SEQ_TOK % tok == 0 and tok % 64 == 0:
            return fused(devices == 16, hidden, *rest)
        return with_collectives(hidden, *rest)

    return jax.shard_map(
        on_device,
        mesh=mesh,
        in_specs=(
            P(("groups", "expert"), None),
            P(),
            P(("groups", "expert"), None),
            P(("groups", "expert"), None),
            P("groups"),
            P("expert", None, None),
            P("expert", None, None),
            P("expert", None, None),
        ),
        out_specs=P(("groups", "expert"), None),
        check_vma=False,
    )
```
